512 devices in a mesh: val: 16 (over x, y_hi, core), cond: 32 (over z, y_lo).
Axes of the slice: x: 4, y: 8 (y_hi: 2, y_lo: 4; y = y_hi * 4 + y_lo), z: 8, core: 2. Of those that a mesh axis runs over, the one named last changes fastest.
Arguments:
- val_orbitals: bfloat16 [64, 768], P('val'), may hold values from -6 to 6
- cond_orbitals: bfloat16 [256, 768], P('cond'), may hold values from -6 to 6
- val_energy: bfloat16 [64], P('val'), may hold values from -0.59765625 to -0.049804688
- cond_energy: bfloat16 [256], P('cond'), may hold values from 0.049804688 to 1.1953125
- wave_index: int32 [4096], P('cond'), may hold values from 0 to 884735
Outputs:
- chi_real: float32 [128, 4096], P('val', 'cond')
- chi_imag: float32 [128, 4096], P('val', 'cond')
The draws below stay inside these ranges and needn't reach their ends.
Inputs may be any that keep to these rules, and one draw needn't show every extreme that they name: `wave_index`: values may repeat.
All inputs are finite; a program needn't handle non-finite values.
Results may differ from the reference program's by a relative error of at most 0.0037.
Values may be sent and summed in bfloat16 or wider, within the bound.
No kernel may reach another device: no remote copies, remote signals or barrier semaphores. Data moves between devices by JAX's collectives and lax.ppermute only.
A program may use at most 64 MiB of HBM per device.

```python
import math
import jax
import jax.numpy as jnp
from jax import lax

NG = 96
NPW = 4096
NW = 128
SLAB_Y = 4
NPTS = 768
NVAL = 64
NCOND = 256


def set_ends(values, own_key, low, high):
    index_at = [jax.random.randint(jax.random.fold_in(own_key, axis), (), 0, length) for axis, length in enumerate(values.shape)]
    widest = values.shape.index(max(values.shape))
    next_to = index_at[:widest] + [(index_at[widest] + 1) % values.shape[widest]] + index_at[widest + 1:]
    return values.at[tuple(index_at)].set(low).at[tuple(next_to)].set(high)


def levels(rng, extent, pieces, low, largest):
    factor_of = 1.0
    for dim, shards_of in pieces:
        draws = jax.random.uniform(jax.random.fold_in(jax.random.fold_in(rng, 6), dim), (shards_of,), jnp.float32, low / len(pieces), largest / len(pieces))
        factor_of = factor_of * jnp.repeat(jnp.exp(draws), extent[dim] // shards_of).reshape((-1,) + (1,) * (len(extent) - 1 - dim))
    return factor_of


def bell_draw(key, shape, scale, limit, cuts=(), held_as=jnp.bfloat16):
    drawn = scale * jax.random.normal(key, shape, jnp.float32)
    if cuts:
        drawn = drawn * levels(key, shape, cuts, -0.22, 0.18)
    return jnp.clip(drawn, -limit, limit).astype(held_as)


def setup_inputs(seed: int = 0) -> dict:
    keys = jax.random.split(jax.random.key(seed), 6)
    return {
        "val_orbitals": bell_draw(keys[0], (NVAL, NPTS), 1.0, 6.0, ((0, 16),)),
        "cond_orbitals": bell_draw(keys[1], (NCOND, NPTS), 1.0, 6.0, ((0, 32),)),
        "val_energy": jnp.clip(-0.59765625 + 0.54785156 * jax.random.uniform(keys[2], (NVAL,), jnp.float32) ** levels(keys[2], (NVAL,), ((0, 16),), -0.2, 0.2), -0.59765625, -0.049804688).astype(jnp.bfloat16),
        "cond_energy": jnp.clip(0.049804688 + 1.1455078 * jax.random.uniform(keys[3], (NCOND,), jnp.float32) ** levels(keys[3], (NCOND,), ((0, 32),), -0.2, 0.2), 0.049804688, 1.1953125).astype(jnp.bfloat16),
        "wave_index": set_ends(jax.random.randint(keys[4], (NPW,), 0, NG * NG * NG), jax.random.fold_in(keys[4], 1), 0, (NG * NG * NG) - 1).astype(jnp.int32),
    }


def phase_table(wave_index, point_count, grid_cells, slab_rows):
    points = lax.iota(jnp.int32, point_count)
    along_x = points % grid_cells
    along_y = points // grid_cells % slab_rows
    along_z = points // (grid_cells * slab_rows)
    wave_x = wave_index // (grid_cells * grid_cells)
    wave_y = wave_index // grid_cells % grid_cells
    wave_z = wave_index % grid_cells
    phase_turns = (along_x[:, None] * wave_x[None, :] + along_y[:, None] * wave_y[None, :] + along_z[:, None] * wave_z[None, :]) % grid_cells
    angles = phase_turns.astype(jnp.float32) * (2.0 * math.pi / grid_cells)
    return jnp.concatenate([jnp.cos(angles), jnp.sin(angles)], axis=1).astype(jnp.bfloat16)

def reference(val_orbitals, cond_orbitals, val_energy, cond_energy, wave_index):
    row_table = phase_table(wave_index, NPTS, NG, SLAB_Y)
    window_table = phase_table(wave_index[:NW], NPTS, NG, SLAB_Y)
    cond_energies = cond_energy.astype(jnp.float32)
    cond_values = cond_orbitals.astype(jnp.float32)

    def one_valence(totals, inputs):
        orbital, energy = inputs
        density = (cond_values * orbital[None, :].astype(jnp.float32)).astype(jnp.bfloat16)
        window_terms = jnp.dot(density, window_table, preferred_element_type=jnp.float32)
        weights = 1.0 / (cond_energies - energy.astype(jnp.float32))
        weighted = window_terms * weights[:, None]
        update = jnp.dot(weighted.T, density.astype(jnp.float32), precision=lax.Precision.HIGHEST)
        return (totals + update, None)
    totals, unused = lax.scan(one_valence, jnp.zeros((2 * NW, NPTS), jnp.float32), (val_orbitals, val_energy))
    products = jnp.dot(totals, row_table.astype(jnp.float32), precision=lax.Precision.HIGHEST)
    factor = -4.0 / math.sqrt(NVAL * NCOND)
    real_part = factor * (products[:NW, :NPW] + products[NW:, NPW:])
    imag_part = factor * (products[:NW, NPW:] - products[NW:, :NPW])
    return (real_part, imag_part)
```

```python
import functools
import math

import jax
import jax.numpy as jnp
from jax import lax
from jax.experimental import pallas as pl
from jax.experimental.pallas import tpu as pltpu
from jax.sharding import PartitionSpec as P

NG = 96
SLAB_Y = 4
NPTS = 768
VMEM = pl.BlockSpec(memory_space=pltpu.VMEM)


def device_number(x, y, z, core):
    val = x * 4 + (y // 4) * 2 + core
    return val * 32 + z * 4 + y % 4


def groups():
    out = []
    for first_y in (2, 6):
        for x0 in range(4):
            for core0 in range(2):
                members = [
                    device_number((z + x0) % 4, (first_y + t) % 8, z, (core0 + z // 4) % 2)
                    for z in range(8)
                    for t in range(4)
                ]
                out.append(sorted(members, key=lambda d: d % 32))
    return out


def whole_part(value, divisor):
    return jnp.floor((value + 0.5) * (1.0 / divisor))


def components(index):
    flat = index.astype(jnp.float32)
    a = whole_part(flat, NG * NG)
    rest = flat - a * (NG * NG)
    b = whole_part(rest, NG)
    return a, b, rest - b * NG


def cos_sin(a, b, c, x, y, z):
    turns = a * x + b * y + c * z
    turns = turns - NG * whole_part(turns, NG)
    angles = turns * (2.0 * math.pi / NG)
    return jnp.cos(angles), jnp.sin(angles)


def grid_points(shape, dim):
    points = lax.broadcasted_iota(jnp.int32, shape, dim).astype(jnp.float32)
    z = whole_part(points, NG * SLAB_Y)
    rest = points - z * (NG * SLAB_Y)
    y = whole_part(rest, NG)
    return rest - y * NG, y, z


def pack_kernel(val_ref, cond_ref, val_energy_ref, cond_energy_ref, index_ref, out_ref):
    odd = lax.rem(lax.axis_index("cond"), 2) == 1
    val = val_ref[...].astype(jnp.float32)
    val = jnp.where(odd, val[2:4], val[0:2])
    a, b, c = components(index_ref[...].reshape(1, 128))
    energy = val_energy_ref[...].astype(jnp.float32)
    energy = jnp.where(odd, energy[:, 2:4], energy[:, 0:2])
    tail = jnp.concatenate(
        [cond_energy_ref[...].astype(jnp.float32), energy, jnp.zeros((1, 118), jnp.float32)], axis=1
    )
    rows = [val[h : h + 1, 256 * q : 256 * q + 256] for h in range(2) for q in range(3)]
    rows += [jnp.concatenate([a, b], axis=1), jnp.concatenate([c, tail], axis=1)]
    side = jnp.concatenate(rows, axis=0)
    block = jnp.concatenate([cond_ref[...].astype(jnp.float32), side], axis=1).astype(jnp.bfloat16)
    for k in range(out_ref.shape[0]):
        out_ref[k] = block


def dot(a, b, dims=(1, 0)):
    return lax.dot_general(
        a, b, (((dims[0],), (dims[1],)), ((), ())), preferred_element_type=jnp.float32
    )


def one_hot(condition):
    return jnp.where(condition, 1.0, 0.0).astype(jnp.bfloat16)


def iotas(rows, cols):
    return (
        lax.broadcasted_iota(jnp.int32, (rows, cols), 0),
        lax.broadcasted_iota(jnp.int32, (rows, cols), 1),
    )


def chi_kernel(factor, got_ref, table_ref, real_ref, imag_ref, left_ref, weighted_ref):
    conduction = got_ref[:, 0:NPTS]
    side = got_ref[:, NPTS:]

    row, lane = iotas(8, 128)
    mine = lane == row + 8 * lax.axis_index("val")
    head = got_ref[0:16, NPTS:].astype(jnp.float32)

    def own(values):
        return jnp.sum(jnp.where(mine, values, 0.0), axis=1, keepdims=True)

    a, b, c = own(head[6:7, 0:128]), own(head[6:7, 128:256]), own(head[7:8, 0:128])
    window = jnp.concatenate(cos_sin(a, b, c, *grid_points((8, NPTS), 1)), axis=0).astype(jnp.bfloat16)
    window = window.astype(jnp.float32)

    v, r = iotas(64, 256)
    first = 8 * (v // 2) + 3 * (v % 2)
    valence = jnp.concatenate([dot(one_hot(r == first + q), side) for q in range(3)], axis=1)
    energies = side[:, 128:256]
    picked = dot(one_hot(r == 8 * (v // 2) + 7), energies)
    v, l = iotas(64, 128)
    val_energy = jnp.sum(jnp.where(l == 8 + v % 2, picked, 0.0), axis=1, keepdims=True)
    r, k = iotas(256, 256)
    spread = dot(energies, one_hot(r == 8 * (k // 8) + 7), (0, 0))
    l, k = iotas(128, 256)
    cond_energy = jnp.sum(jnp.where(l == k % 8, spread, 0.0), axis=0, keepdims=True)
    weights = factor / (cond_energy - val_energy)

    for j in range(16):
        left_ref[64 * j : 64 * j + 64, :] = (valence * window[j : j + 1, :]).astype(jnp.bfloat16)
    terms = dot(left_ref[...], conduction, (1, 1))
    for j in range(16):
        weighted_ref[64 * j : 64 * j + 64, :] = (terms[64 * j : 64 * j + 64, :] * weights).astype(jnp.bfloat16)
    back = dot(weighted_ref[...], conduction)
    totals = jnp.concatenate(
        [jnp.sum(back[64 * j : 64 * j + 64, :] * valence, axis=0, keepdims=True) for j in range(16)], axis=0
    )
    high = totals.astype(jnp.bfloat16)
    low = (totals - high.astype(jnp.float32)).astype(jnp.bfloat16)
    products = dot(high, table_ref[...]) + dot(low, table_ref[...])
    real_ref[...] = products[0:8, 0:128] + products[8:16, 128:256]
    imag_ref[...] = products[0:8, 128:256] - products[8:16, 0:128]


def table_kernel(index_ref, out_ref):
    a, b, c = components(index_ref[...].reshape(1, 128))
    cos, sin = cos_sin(a, b, c, *grid_points((NPTS, 1), 0))
    out_ref[:, 0:128] = cos.astype(jnp.bfloat16)
    out_ref[:, 128:256] = sin.astype(jnp.bfloat16)


def pack(val, cond, val_energy, cond_energy, index):
    return pl.pallas_call(
        pack_kernel,
        out_shape=jax.ShapeDtypeStruct((32, 8, 1024), jnp.bfloat16),
        in_specs=[VMEM] * 5,
        out_specs=VMEM,
    )(val, cond, val_energy, cond_energy, index)


def table(index):
    return pl.pallas_call(
        table_kernel,
        out_shape=jax.ShapeDtypeStruct((NPTS, 256), jnp.bfloat16),
        in_specs=[VMEM],
        out_specs=VMEM,
        cost_estimate=pl.CostEstimate(flops=20_000_000, bytes_accessed=400_000, transcendentals=200_000),
    )(index)


def chi(got, row_table, factor):
    return pl.pallas_call(
        functools.partial(chi_kernel, factor),
        out_shape=[jax.ShapeDtypeStruct((8, 128), jnp.float32)] * 2,
        in_specs=[VMEM] * 2,
        out_specs=[VMEM] * 2,
        scratch_shapes=[pltpu.VMEM((1024, NPTS), jnp.bfloat16), pltpu.VMEM((1024, 256), jnp.bfloat16)],
        compiler_params=pltpu.CompilerParams(vmem_limit_bytes=32 * 1024 * 1024),
    )(got, row_table)


def per_device(val_orbitals, cond_orbitals, val_energy, cond_energy, wave_index):
    factor = -4.0 / math.sqrt(4 * lax.axis_size("val") * 8 * lax.axis_size("cond"))
    sent = pack(
        val_orbitals, cond_orbitals, val_energy.reshape(1, 4), cond_energy.reshape(1, 8), wave_index.reshape(1, 128)
    )
    got = lax.all_to_all(sent, ("val", "cond"), 0, 0, tiled=True, axis_index_groups=groups())
    row_table = table(wave_index.reshape(1, 128))
    return tuple(chi(got.reshape(256, 1024), row_table, factor))


def solution(mesh):
    return jax.shard_map(
        per_device,
        mesh=mesh,
        in_specs=(P("val", None), P("cond", None), P("val"), P("cond"), P("cond")),
        out_specs=(P("val", "cond"), P("val", "cond")),
        check_vma=False,
    )
```

```python
import functools
import math

import jax
import jax.numpy as jnp
from jax import lax
from jax.experimental import pallas as pl
from jax.experimental.pallas import tpu as pltpu
from jax.sharding import PartitionSpec as P

NG = 96
SLAB_Y = 4
NPTS = 768
VMEM = pl.BlockSpec(memory_space=pltpu.VMEM)


def device_number(x, y, z, core):
    val = x * 4 + (y // 4) * 2 + core
    return val * 32 + z * 4 + y % 4


def groups():
    out = []
    for first_y in (2, 6):
        for x0 in range(4):
            for core0 in range(2):
                members = [
                    device_number((z + x0) % 4, (first_y + t) % 8, z, (core0 + z // 4) % 2)
                    for z in range(8)
                    for t in range(4)
                ]
                out.append(sorted(members, key=lambda d: d % 32))
    return out


def whole_part(value, divisor):
    return jnp.floor((value + 0.5) * (1.0 / divisor))


def components(index):
    flat = index.astype(jnp.float32)
    a = whole_part(flat, NG * NG)
    rest = flat - a * (NG * NG)
    b = whole_part(rest, NG)
    return a, b, rest - b * NG


def cos_sin(a, b, c, x, y, z):
    turns = a * x + b * y + c * z
    turns = turns - NG * whole_part(turns, NG)
    angles = turns * (2.0 * math.pi / NG)
    return jnp.cos(angles), jnp.sin(angles)


def grid_points(shape, dim):
    points = lax.broadcasted_iota(jnp.int32, shape, dim).astype(jnp.float32)
    z = whole_part(points, NG * SLAB_Y)
    rest = points - z * (NG * SLAB_Y)
    y = whole_part(rest, NG)
    return rest - y * NG, y, z


def pack_kernel(val_ref, cond_ref, val_energy_ref, cond_energy_ref, index_ref, out_ref):
    odd = lax.rem(lax.axis_index("cond"), 2) == 1
    val = val_ref[...].astype(jnp.float32)
    val = jnp.where(odd, val[2:4], val[0:2])
    a, b, c = components(index_ref[...].reshape(1, 128))
    energy = val_energy_ref[...].astype(jnp.float32)
    energy = jnp.where(odd, energy[:, 2:4], energy[:, 0:2])
    tail = jnp.concatenate(
        [cond_energy_ref[...].astype(jnp.float32), energy, jnp.zeros((1, 118), jnp.float32)], axis=1
    )
    rows = [val[h : h + 1, 256 * q : 256 * q + 256] for h in range(2) for q in range(3)]
    rows += [jnp.concatenate([a, b], axis=1), jnp.concatenate([c, tail], axis=1)]
    side = jnp.concatenate(rows, axis=0)
    block = jnp.concatenate([cond_ref[...].astype(jnp.float32), side], axis=1).astype(jnp.bfloat16)
    for k in range(out_ref.shape[0]):
        out_ref[k] = block


def dot(a, b, dims=(1, 0)):
    return lax.dot_general(
        a, b, (((dims[0],), (dims[1],)), ((), ())), preferred_element_type=jnp.float32
    )


def one_hot(condition):
    return jnp.where(condition, 1.0, 0.0).astype(jnp.bfloat16)


def iotas(rows, cols):
    return (
        lax.broadcasted_iota(jnp.int32, (rows, cols), 0),
        lax.broadcasted_iota(jnp.int32, (rows, cols), 1),
    )


def chi_kernel(factor, got_ref, table_ref, real_ref, imag_ref, left_ref, weighted_ref):
    conduction = got_ref[:, 0:NPTS]
    side = got_ref[:, NPTS:]

    row, lane = iotas(8, 128)
    mine = lane == row + 8 * lax.axis_index("val")
    head = got_ref[0:16, NPTS:].astype(jnp.float32)

    def own(values):
        return jnp.sum(jnp.where(mine, values, 0.0), axis=1, keepdims=True)

    a, b, c = own(head[6:7, 0:128]), own(head[6:7, 128:256]), own(head[7:8, 0:128])
    window = jnp.concatenate(cos_sin(a, b, c, *grid_points((8, NPTS), 1)), axis=0).astype(jnp.bfloat16)
    window = window.astype(jnp.float32)

    v, r = iotas(64, 256)
    first = 8 * (v // 2) + 3 * (v % 2)
    valence = jnp.concatenate([dot(one_hot(r == first + q), side) for q in range(3)], axis=1)
    energies = side[:, 128:256]
    picked = dot(one_hot(r == 8 * (v // 2) + 7), energies)
    v, l = iotas(64, 128)
    val_energy = jnp.sum(jnp.where(l == 8 + v % 2, picked, 0.0), axis=1, keepdims=True)
    r, k = iotas(256, 256)
    spread = dot(energies, one_hot(r == 8 * (k // 8) + 7), (0, 0))
    l, k = iotas(128, 256)
    cond_energy = jnp.sum(jnp.where(l == k % 8, spread, 0.0), axis=0, keepdims=True)
    weights = factor / (cond_energy - val_energy)

    for j in range(16):
        left_ref[64 * j : 64 * j + 64, :] = (valence * window[j : j + 1, :]).astype(jnp.bfloat16)
    terms = dot(left_ref[...], conduction, (1, 1))
    for j in range(16):
        weighted_ref[64 * j : 64 * j + 64, :] = (terms[64 * j : 64 * j + 64, :] * weights).astype(jnp.bfloat16)
    back = dot(weighted_ref[...], conduction)
    totals = jnp.concatenate(
        [jnp.sum(back[64 * j : 64 * j + 64, :] * valence, axis=0, keepdims=True) for j in range(16)], axis=0
    )
    high = totals.astype(jnp.bfloat16)
    low = (totals - high.astype(jnp.float32)).astype(jnp.bfloat16)
    products = dot(high, table_ref[...]) + dot(low, table_ref[...])
    real_ref[...] = products[0:8, 0:128] + products[8:16, 128:256]
    imag_ref[...] = products[0:8, 128:256] - products[8:16, 0:128]


def table_kernel(index_ref, out_ref):
    a, b, c = components(index_ref[...].reshape(1, 128))
    cos, sin = cos_sin(a, b, c, *grid_points((NPTS, 1), 0))
    out_ref[:, 0:128] = cos.astype(jnp.bfloat16)
    out_ref[:, 128:256] = sin.astype(jnp.bfloat16)


def pack(val, cond, val_energy, cond_energy, index):
    return pl.pallas_call(
        pack_kernel,
        out_shape=pltpu.VMEM((32, 8, 1024), jnp.bfloat16),
        in_specs=[VMEM] * 5,
        out_specs=VMEM,
    )(val, cond, val_energy, cond_energy, index)


def table(index):
    return pl.pallas_call(
        table_kernel,
        out_shape=pltpu.VMEM((NPTS, 256), jnp.bfloat16),
        in_specs=[VMEM],
        out_specs=VMEM,
        cost_estimate=pl.CostEstimate(flops=20_000_000, bytes_accessed=400_000, transcendentals=200_000),
    )(index)


def chi(got, row_table, factor):
    return pl.pallas_call(
        functools.partial(chi_kernel, factor),
        out_shape=[jax.ShapeDtypeStruct((8, 128), jnp.float32)] * 2,
        in_specs=[VMEM] * 2,
        out_specs=[VMEM] * 2,
        scratch_shapes=[pltpu.VMEM((1024, NPTS), jnp.bfloat16), pltpu.VMEM((1024, 256), jnp.bfloat16)],
        compiler_params=pltpu.CompilerParams(vmem_limit_bytes=32 * 1024 * 1024),
    )(got, row_table)


def per_device(val_orbitals, cond_orbitals, val_energy, cond_energy, wave_index):
    factor = -4.0 / math.sqrt(4 * lax.axis_size("val") * 8 * lax.axis_size("cond"))
    sent = pack(
        val_orbitals, cond_orbitals, val_energy.reshape(1, 4), cond_energy.reshape(1, 8), wave_index.reshape(1, 128)
    )
    got = lax.all_to_all(sent, ("val", "cond"), 0, 0, tiled=True, axis_index_groups=groups())
    row_table = table(wave_index.reshape(1, 128))
    return tuple(chi(got.reshape(256, 1024), row_table, factor))


def solution(mesh):
    return jax.shard_map(
        per_device,
        mesh=mesh,
        in_specs=(P("val", None), P("cond", None), P("val"), P("cond"), P("cond")),
        out_specs=(P("val", "cond"), P("val", "cond")),
        check_vma=False,
    )
```

```python
import functools
import math

import jax
import jax.numpy as jnp
from jax import lax
from jax.experimental import pallas as pl
from jax.experimental.pallas import tpu as pltpu
from jax.sharding import PartitionSpec as P

NG = 96
SLAB_Y = 4
NPTS = 768
VMEM = pl.BlockSpec(memory_space=pltpu.VMEM)


def device_number(x, y, z, core):
    val = x * 4 + (y // 4) * 2 + core
    return val * 32 + z * 4 + y % 4


def groups():
    out = []
    for first_y in (2, 6):
        for x0 in range(4):
            for core in range(2):
                members = [
                    device_number((z + x0) % 4, (first_y + t) % 8, z, core)
                    for z in range(8)
                    for t in range(4)
                ]
                out.append(sorted(members, key=lambda d: d % 32))
    return out


def whole_part(value, divisor):
    return jnp.floor((value + 0.5) * (1.0 / divisor))


def components(index):
    flat = index.astype(jnp.float32)
    a = whole_part(flat, NG * NG)
    rest = flat - a * (NG * NG)
    b = whole_part(rest, NG)
    return a, b, rest - b * NG


def cos_sin(a, b, c, x, y, z):
    turns = a * x + b * y + c * z
    turns = turns - NG * whole_part(turns, NG)
    angles = turns * (2.0 * math.pi / NG)
    return jnp.cos(angles), jnp.sin(angles)


def grid_points(shape, dim):
    points = lax.broadcasted_iota(jnp.int32, shape, dim).astype(jnp.float32)
    z = whole_part(points, NG * SLAB_Y)
    rest = points - z * (NG * SLAB_Y)
    y = whole_part(rest, NG)
    return rest - y * NG, y, z


def dot(a, b, dims=(1, 0)):
    return lax.dot_general(
        a, b, (((dims[0],), (dims[1],)), ((), ())), preferred_element_type=jnp.float32
    )


def one_hot(condition):
    return jnp.where(condition, 1.0, 0.0).astype(jnp.bfloat16)


def iotas(rows, cols):
    return (
        lax.broadcasted_iota(jnp.int32, (rows, cols), 0),
        lax.broadcasted_iota(jnp.int32, (rows, cols), 1),
    )


def pack_kernel(val_ref, cond_ref, val_energy_ref, cond_energy_ref, index_ref, out_ref):
    cond = lax.axis_index("cond")
    share = 2 * (cond // 16) + lax.rem(cond, 2)
    row, lane = iotas(4, NPTS)
    val = jnp.sum(jnp.where(row == share, val_ref[...].astype(jnp.float32), 0.0), axis=0, keepdims=True)
    a, b, c = components(index_ref[...].reshape(1, 128))
    row, lane = iotas(1, 4)
    energy = jnp.sum(jnp.where(lane == share, val_energy_ref[...].astype(jnp.float32), 0.0), axis=1, keepdims=True)
    tail = jnp.concatenate(
        [cond_energy_ref[...].astype(jnp.float32), energy, jnp.zeros((1, 119), jnp.float32)], axis=1
    )
    rows = [val[:, 256 * q : 256 * q + 256] for q in range(3)]
    rows += [jnp.concatenate([a, b], axis=1), jnp.concatenate([c, tail], axis=1), jnp.zeros((3, 256), jnp.float32)]
    side = jnp.concatenate(rows, axis=0)
    block = jnp.concatenate([cond_ref[...].astype(jnp.float32), side], axis=1).astype(jnp.bfloat16)
    for k in range(out_ref.shape[0]):
        out_ref[k] = block


def chi_kernel(factor, got_ref, table_ref, mine_ref, other_ref, left_ref, weighted_ref):
    conduction = got_ref[:, 0:NPTS]
    side = got_ref[:, NPTS:]

    val = lax.axis_index("val")
    row, lane = iotas(16, 128)
    mine = lane == row + 16 * (val // 2)
    head = got_ref[0:16, NPTS:].astype(jnp.float32)

    def own(values):
        return jnp.sum(jnp.where(mine, values, 0.0), axis=1, keepdims=True)

    a, b, c = own(head[3:4, 0:128]), own(head[3:4, 128:256]), own(head[4:5, 0:128])
    window = jnp.concatenate(cos_sin(a, b, c, *grid_points((16, NPTS), 1)), axis=0).astype(jnp.bfloat16)
    window = window.astype(jnp.float32)

    v, r = iotas(32, 256)
    valence = jnp.concatenate([dot(one_hot(r == 8 * v + q), side) for q in range(3)], axis=1)
    energies = side[:, 128:256]
    picked = dot(one_hot(r == 8 * v + 4), energies)
    v, l = iotas(32, 128)
    val_energy = jnp.sum(jnp.where(l == 8, picked, 0.0), axis=1, keepdims=True)
    r, k = iotas(256, 256)
    spread = dot(energies, one_hot(r == 8 * (k // 8) + 4), (0, 0))
    l, k = iotas(128, 256)
    cond_energy = jnp.sum(jnp.where(l == k % 8, spread, 0.0), axis=0, keepdims=True)
    weights = factor / (cond_energy - val_energy)

    for j in range(32):
        left_ref[32 * j : 32 * j + 32, :] = (valence * window[j : j + 1, :]).astype(jnp.bfloat16)
    terms = dot(left_ref[...], conduction, (1, 1))
    for j in range(32):
        weighted_ref[32 * j : 32 * j + 32, :] = (terms[32 * j : 32 * j + 32, :] * weights).astype(jnp.bfloat16)
    back = dot(weighted_ref[...], conduction)
    totals = jnp.concatenate(
        [jnp.sum(back[32 * j : 32 * j + 32, :] * valence, axis=0, keepdims=True) for j in range(32)], axis=0
    )
    high = totals.astype(jnp.bfloat16)
    low = (totals - high.astype(jnp.float32)).astype(jnp.bfloat16)
    products = dot(high, table_ref[...]) + dot(low, table_ref[...])
    real = products[0:16, 0:128] + products[16:32, 128:256]
    imag = products[0:16, 128:256] - products[16:32, 0:128]
    both = jnp.concatenate([real, imag], axis=1)
    first = lax.rem(val, 2) == 0
    mine_ref[...] = jnp.where(first, both[0:8], both[8:16])
    other_ref[...] = jnp.where(first, both[8:16], both[0:8])


def table_kernel(index_ref, out_ref):
    a, b, c = components(index_ref[...].reshape(1, 128))
    cos, sin = cos_sin(a, b, c, *grid_points((NPTS, 1), 0))
    out_ref[:, 0:128] = cos.astype(jnp.bfloat16)
    out_ref[:, 128:256] = sin.astype(jnp.bfloat16)


def pack(val, cond, val_energy, cond_energy, index):
    return pl.pallas_call(
        pack_kernel,
        out_shape=pltpu.VMEM((32, 8, 1024), jnp.bfloat16),
        in_specs=[VMEM] * 5,
        out_specs=VMEM,
    )(val, cond, val_energy, cond_energy, index)


def table(index):
    return pl.pallas_call(
        table_kernel,
        out_shape=pltpu.VMEM((NPTS, 256), jnp.bfloat16),
        in_specs=[VMEM],
        out_specs=VMEM,
        cost_estimate=pl.CostEstimate(flops=20_000_000, bytes_accessed=400_000, transcendentals=200_000),
    )(index)


def chi(got, row_table, factor):
    return pl.pallas_call(
        functools.partial(chi_kernel, factor),
        out_shape=[jax.ShapeDtypeStruct((8, 256), jnp.float32)] * 2,
        in_specs=[VMEM] * 2,
        out_specs=[VMEM] * 2,
        scratch_shapes=[pltpu.VMEM((1024, NPTS), jnp.bfloat16), pltpu.VMEM((1024, 256), jnp.bfloat16)],
        compiler_params=pltpu.CompilerParams(vmem_limit_bytes=32 * 1024 * 1024),
    )(got, row_table)


def per_device(val_orbitals, cond_orbitals, val_energy, cond_energy, wave_index):
    factor = -4.0 / math.sqrt(4 * lax.axis_size("val") * 8 * lax.axis_size("cond"))
    sent = pack(
        val_orbitals, cond_orbitals, val_energy.reshape(1, 4), cond_energy.reshape(1, 8), wave_index.reshape(1, 128)
    )
    got = lax.all_to_all(sent, ("val", "cond"), 0, 0, tiled=True, axis_index_groups=groups())
    row_table = table(wave_index.reshape(1, 128))
    mine, other = chi(got.reshape(256, 1024), row_table, factor)
    theirs = lax.ppermute(other, "val", [(i, i ^ 1) for i in range(16)])
    return tuple(jnp.split(mine + theirs, 2, axis=1))


def solution(mesh):
    return jax.shard_map(
        per_device,
        mesh=mesh,
        in_specs=(P("val", None), P("cond", None), P("val"), P("cond"), P("cond")),
        out_specs=(P("val", "cond"), P("val", "cond")),
        check_vma=False,
    )
```

```python
import functools
import math

import jax
import jax.numpy as jnp
from jax import lax
from jax.experimental import pallas as pl
from jax.experimental.pallas import tpu as pltpu
from jax.sharding import PartitionSpec as P

NG = 96
SLAB_Y = 4
NPTS = 768
STEP = 4
VMEM = pl.BlockSpec(memory_space=pltpu.VMEM)


def device_number(x, y, z, core):
    val = x * 4 + (y // 4) * 2 + core
    return val * 32 + z * 4 + y % 4


def groups():
    out = []
    for first_y in (2, 6):
        for x0 in range(4):
            for core0 in range(2):
                members = [
                    device_number((z + x0) % 4, (first_y + t) % 8, z, (core0 + z // 4) % 2)
                    for z in range(8)
                    for t in range(4)
                ]
                out.append(sorted(members, key=lambda d: d % 32))
    return out


def whole_part(value, divisor):
    return jnp.floor((value + 0.5) * (1.0 / divisor))


def components(index):
    flat = index.astype(jnp.float32)
    a = whole_part(flat, NG * NG)
    rest = flat - a * (NG * NG)
    b = whole_part(rest, NG)
    return a, b, rest - b * NG


def cos_sin(a, b, c, x, y, z):
    turns = a * x + b * y + c * z
    turns = turns - NG * whole_part(turns, NG)
    angles = turns * (2.0 * math.pi / NG)
    return jnp.cos(angles), jnp.sin(angles)


def grid_points(shape, dim):
    points = lax.broadcasted_iota(jnp.int32, shape, dim).astype(jnp.float32)
    z = whole_part(points, NG * SLAB_Y)
    rest = points - z * (NG * SLAB_Y)
    y = whole_part(rest, NG)
    return rest - y * NG, y, z


def pack_kernel(val_ref, cond_ref, val_energy_ref, cond_energy_ref, index_ref, out_ref):
    odd = lax.rem(lax.axis_index("cond"), 2) == 1
    val = val_ref[...].astype(jnp.float32)
    val = jnp.where(odd, val[2:4], val[0:2])
    a, b, c = components(index_ref[...].reshape(1, 128))
    energy = val_energy_ref[...].astype(jnp.float32)
    energy = jnp.where(odd, energy[:, 2:4], energy[:, 0:2])
    tail = jnp.concatenate(
        [cond_energy_ref[...].astype(jnp.float32), energy, jnp.zeros((1, 118), jnp.float32)], axis=1
    )
    rows = [val[h : h + 1, 256 * q : 256 * q + 256] for h in range(2) for q in range(3)]
    rows += [jnp.concatenate([a, b], axis=1), jnp.concatenate([c, tail], axis=1)]
    side = jnp.concatenate(rows, axis=0)
    block = jnp.concatenate([cond_ref[...].astype(jnp.float32), side], axis=1).astype(jnp.bfloat16)
    for k in range(out_ref.shape[0]):
        out_ref[k] = block


def dot(a, b, dims=(1, 0)):
    return lax.dot_general(
        a, b, (((dims[0],), (dims[1],)), ((), ())), preferred_element_type=jnp.float32
    )


def one_hot(condition):
    return jnp.where(condition, 1.0, 0.0).astype(jnp.bfloat16)


def iotas(rows, cols):
    return (
        lax.broadcasted_iota(jnp.int32, (rows, cols), 0),
        lax.broadcasted_iota(jnp.int32, (rows, cols), 1),
    )


def phase_table(index):
    a, b, c = components(index)
    x = lax.broadcasted_iota(jnp.int32, (NG, 1), 0).astype(jnp.float32)
    cos_x, sin_x = cos_sin(a, b, c, x, 0.0, 0.0)
    line = lax.broadcasted_iota(jnp.int32, (NPTS // NG, 1), 0).astype(jnp.float32)
    z = whole_part(line, SLAB_Y)
    cos_l, sin_l = cos_sin(a, b, c, 0.0, line - z * SLAB_Y, z)
    blocks = []
    for k in range(NPTS // NG):
        ck, sk = cos_l[k : k + 1], sin_l[k : k + 1]
        blocks.append(jnp.concatenate([cos_x * ck - sin_x * sk, sin_x * ck + cos_x * sk], axis=1).astype(jnp.bfloat16))
    return jnp.concatenate(blocks, axis=0)


def chi_kernel(factor, got_ref, index_ref, real_ref, imag_ref):
    conduction = got_ref[:, 0:NPTS]
    side = got_ref[:, NPTS:]

    row, lane = iotas(8, 128)
    mine = lane == row + 8 * lax.axis_index("val")
    head = got_ref[0:16, NPTS:].astype(jnp.float32)

    def own(values):
        return jnp.sum(jnp.where(mine, values, 0.0), axis=1, keepdims=True)

    a, b, c = own(head[6:7, 0:128]), own(head[6:7, 128:256]), own(head[7:8, 0:128])
    window = jnp.concatenate(cos_sin(a, b, c, *grid_points((8, NPTS), 1)), axis=0).astype(jnp.bfloat16)

    v, r = iotas(64, 256)
    first = 8 * (v // 2) + 3 * (v % 2)
    valence = jnp.concatenate([dot(one_hot(r == first + q), side) for q in range(3)], axis=1)
    narrow = valence.astype(jnp.bfloat16)
    energies = side[:, 128:256]
    picked = dot(one_hot(r == 8 * (v // 2) + 7), energies)
    v, l = iotas(64, 128)
    val_energy = jnp.sum(jnp.where(l == 8 + v % 2, picked, 0.0), axis=1, keepdims=True)
    r, k = iotas(256, 256)
    spread = dot(energies, one_hot(r == 8 * (k // 8) + 7), (0, 0))
    l, k = iotas(128, 256)
    cond_energy = jnp.sum(jnp.where(l == k % 8, spread, 0.0), axis=0, keepdims=True)
    weights = factor / (cond_energy - val_energy)

    totals = []
    for start in range(0, 16, STEP):
        left = jnp.concatenate([narrow * window[j : j + 1, :] for j in range(start, start + STEP)], axis=0)
        terms = dot(left, conduction, (1, 1))
        weighted = [(terms[64 * i : 64 * i + 64] * weights).astype(jnp.bfloat16) for i in range(STEP)]
        back = dot(jnp.concatenate(weighted, axis=0), conduction)
        totals += [jnp.sum(back[64 * i : 64 * i + 64] * valence, axis=0, keepdims=True) for i in range(STEP)]
    totals = jnp.concatenate(totals, axis=0)

    table = phase_table(index_ref[...])
    high = totals.astype(jnp.bfloat16)
    low = (totals - high.astype(jnp.float32)).astype(jnp.bfloat16)
    products = dot(high, table) + dot(low, table)
    real_ref[...] = products[0:8, 0:128] + products[8:16, 128:256]
    imag_ref[...] = products[0:8, 128:256] - products[8:16, 0:128]


def pack(val, cond, val_energy, cond_energy, index):
    return pl.pallas_call(
        pack_kernel,
        out_shape=pltpu.VMEM((32, 8, 1024), jnp.bfloat16),
        in_specs=[VMEM] * 5,
        out_specs=VMEM,
    )(val, cond, val_energy, cond_energy, index)


def chi(got, index, factor):
    return pl.pallas_call(
        functools.partial(chi_kernel, factor),
        out_shape=[jax.ShapeDtypeStruct((8, 128), jnp.float32)] * 2,
        in_specs=[VMEM] * 2,
        out_specs=[VMEM] * 2,
        compiler_params=pltpu.CompilerParams(vmem_limit_bytes=32 * 1024 * 1024),
    )(got, index)


def per_device(val_orbitals, cond_orbitals, val_energy, cond_energy, wave_index):
    factor = -4.0 / math.sqrt(4 * lax.axis_size("val") * 8 * lax.axis_size("cond"))
    sent = pack(
        val_orbitals, cond_orbitals, val_energy.reshape(1, 4), cond_energy.reshape(1, 8), wave_index.reshape(1, 128)
    )
    got = lax.all_to_all(sent, ("val", "cond"), 0, 0, tiled=True, axis_index_groups=groups())
    return tuple(chi(got.reshape(256, 1024), wave_index.reshape(1, 128), factor))


def solution(mesh):
    return jax.shard_map(
        per_device,
        mesh=mesh,
        in_specs=(P("val", None), P("cond", None), P("val"), P("cond"), P("cond")),
        out_specs=(P("val", "cond"), P("val", "cond")),
        check_vma=False,
    )
```

```python
import functools
import math

import jax
import jax.numpy as jnp
from jax import lax
from jax.experimental import pallas as pl
from jax.experimental.pallas import tpu as pltpu
from jax.sharding import PartitionSpec as P

NG = 96
SLAB_Y = 4
NPTS = 768
STEP = 8
VMEM = pl.BlockSpec(memory_space=pltpu.VMEM)


def device_number(x, y, z, core):
    val = x * 4 + (y // 4) * 2 + core
    return val * 32 + z * 4 + y % 4


def groups():
    out = []
    for first_y in (2, 6):
        for x0 in range(4):
            for core0 in range(2):
                members = [
                    device_number((z + x0) % 4, (first_y + t) % 8, z, (core0 + t) % 2)
                    for z in range(8)
                    for t in range(4)
                ]
                out.append(sorted(members, key=lambda d: d % 32))
    return out


def whole_part(value, divisor):
    return jnp.floor((value + 0.5) * (1.0 / divisor))


def components(index):
    flat = index.astype(jnp.float32)
    a = whole_part(flat, NG * NG)
    rest = flat - a * (NG * NG)
    b = whole_part(rest, NG)
    return a, b, rest - b * NG


def cos_sin(a, b, c, x, y, z):
    turns = a * x + b * y + c * z
    turns = turns - NG * whole_part(turns, NG)
    angles = turns * (2.0 * math.pi / NG)
    return jnp.cos(angles), jnp.sin(angles)


def grid_points(shape, dim):
    points = lax.broadcasted_iota(jnp.int32, shape, dim).astype(jnp.float32)
    z = whole_part(points, NG * SLAB_Y)
    rest = points - z * (NG * SLAB_Y)
    y = whole_part(rest, NG)
    return rest - y * NG, y, z


def pack_kernel(val_ref, cond_ref, val_energy_ref, cond_energy_ref, index_ref, out_ref, own_ref):
    upper = lax.axis_index("cond") >= 16
    val = val_ref[...].astype(jnp.float32)
    val = jnp.where(upper, val[2:4], val[0:2])
    a, b, c = components(index_ref[...])
    own_ref[...] = jnp.concatenate([a, b, c, jnp.zeros((5, 128), jnp.float32)], axis=0)
    energy = val_energy_ref[...].astype(jnp.float32)
    energy = jnp.where(upper, energy[:, 2:4], energy[:, 0:2])
    tail = jnp.concatenate(
        [cond_energy_ref[...].astype(jnp.float32), energy, jnp.zeros((1, 118), jnp.float32)], axis=1
    )
    rows = [val[h : h + 1, 256 * q : 256 * q + 256] for h in range(2) for q in range(3)]
    rows += [jnp.concatenate([a, b], axis=1), jnp.concatenate([c, tail], axis=1)]
    side = jnp.concatenate(rows, axis=0)
    block = jnp.concatenate([cond_ref[...].astype(jnp.float32), side], axis=1).astype(jnp.bfloat16)
    for k in range(out_ref.shape[0]):
        out_ref[k] = block


def dot(a, b, dims=(1, 0)):
    return lax.dot_general(
        a, b, (((dims[0],), (dims[1],)), ((), ())), preferred_element_type=jnp.float32
    )


def one_hot(condition):
    return jnp.where(condition, 1.0, 0.0).astype(jnp.bfloat16)


def iotas(rows, cols):
    return (
        lax.broadcasted_iota(jnp.int32, (rows, cols), 0),
        lax.broadcasted_iota(jnp.int32, (rows, cols), 1),
    )


def phase_table(a, b, c):
    x = lax.broadcasted_iota(jnp.int32, (NG, 1), 0).astype(jnp.float32)
    cos_x, sin_x = cos_sin(a, b, c, x, 0.0, 0.0)
    line = lax.broadcasted_iota(jnp.int32, (NPTS // NG, 1), 0).astype(jnp.float32)
    z = whole_part(line, SLAB_Y)
    cos_l, sin_l = cos_sin(a, b, c, 0.0, line - z * SLAB_Y, z)
    blocks = []
    for k in range(NPTS // NG):
        ck, sk = cos_l[k : k + 1], sin_l[k : k + 1]
        blocks.append(jnp.concatenate([cos_x * ck - sin_x * sk, sin_x * ck + cos_x * sk], axis=1).astype(jnp.bfloat16))
    return jnp.concatenate(blocks, axis=0)


def chi_kernel(factor, got_ref, own_ref, real_ref, imag_ref):
    conduction = got_ref[:, 0:NPTS]
    side = got_ref[:, NPTS:]

    row, lane = iotas(8, 128)
    mine = lane == row + 8 * lax.axis_index("val")
    head = got_ref[0:16, NPTS:].astype(jnp.float32)

    def own(values):
        return jnp.sum(jnp.where(mine, values, 0.0), axis=1, keepdims=True)

    a, b, c = own(head[6:7, 0:128]), own(head[6:7, 128:256]), own(head[7:8, 0:128])
    window = jnp.concatenate(cos_sin(a, b, c, *grid_points((8, NPTS), 1)), axis=0).astype(jnp.bfloat16)

    v, r = iotas(64, 256)
    first = 8 * (v // 2) + 3 * (v % 2)
    valence = jnp.concatenate([dot(one_hot(r == first + q), side) for q in range(3)], axis=1)
    narrow = valence.astype(jnp.bfloat16)
    energies = side[:, 128:256]
    picked = dot(one_hot(r == 8 * (v // 2) + 7), energies)
    v, l = iotas(64, 128)
    val_energy = jnp.sum(jnp.where(l == 8 + v % 2, picked, 0.0), axis=1, keepdims=True)
    r, k = iotas(256, 256)
    spread = dot(energies, one_hot(r == 8 * (k // 8) + 7), (0, 0))
    l, k = iotas(128, 256)
    cond_energy = jnp.sum(jnp.where(l == k % 8, spread, 0.0), axis=0, keepdims=True)
    weights = factor / (cond_energy - val_energy)

    lefts = [
        jnp.concatenate([narrow * window[j : j + 1, :] for j in range(start, start + STEP)], axis=0)
        for start in range(0, 16, STEP)
    ]
    totals = []
    ahead = dot(lefts[0], conduction, (1, 1))
    for following in [*lefts[1:], None]:
        terms = ahead
        if following is not None:
            ahead = dot(following, conduction, (1, 1))
        weighted = [(terms[64 * i : 64 * i + 64] * weights).astype(jnp.bfloat16) for i in range(STEP)]
        back = dot(jnp.concatenate(weighted, axis=0), conduction)
        totals += [jnp.sum(back[64 * i : 64 * i + 64] * valence, axis=0, keepdims=True) for i in range(STEP)]
    totals = jnp.concatenate(totals, axis=0)

    table = phase_table(own_ref[0:1], own_ref[1:2], own_ref[2:3])
    high = totals.astype(jnp.bfloat16)
    low = (totals - high.astype(jnp.float32)).astype(jnp.bfloat16)
    products = dot(high, table) + dot(low, table)
    real_ref[...] = products[0:8, 0:128] + products[8:16, 128:256]
    imag_ref[...] = products[0:8, 128:256] - products[8:16, 0:128]


def pack(val, cond, val_energy, cond_energy, index):
    return pl.pallas_call(
        pack_kernel,
        out_shape=[pltpu.VMEM((32, 8, 1024), jnp.bfloat16), pltpu.VMEM((8, 128), jnp.float32)],
        in_specs=[VMEM] * 5,
        out_specs=[VMEM] * 2,
    )(val, cond, val_energy, cond_energy, index)


def chi(got, own, factor):
    return pl.pallas_call(
        functools.partial(chi_kernel, factor),
        out_shape=[jax.ShapeDtypeStruct((8, 128), jnp.float32)] * 2,
        in_specs=[VMEM] * 2,
        out_specs=[VMEM] * 2,
        compiler_params=pltpu.CompilerParams(vmem_limit_bytes=32 * 1024 * 1024),
    )(got, own)


def per_device(val_orbitals, cond_orbitals, val_energy, cond_energy, wave_index):
    factor = -4.0 / math.sqrt(4 * lax.axis_size("val") * 8 * lax.axis_size("cond"))
    sent, own = pack(
        val_orbitals, cond_orbitals, val_energy.reshape(1, 4), cond_energy.reshape(1, 8), wave_index.reshape(1, 128)
    )
    got = lax.all_to_all(sent, ("val", "cond"), 0, 0, tiled=True, axis_index_groups=groups())
    return tuple(chi(got.reshape(256, 1024), own, factor))


def solution(mesh):
    return jax.shard_map(
        per_device,
        mesh=mesh,
        in_specs=(P("val", None), P("cond", None), P("val"), P("cond"), P("cond")),
        out_specs=(P("val", "cond"), P("val", "cond")),
        check_vma=False,
    )
```

```python
import functools
import math

import jax
import jax.numpy as jnp
from jax import lax
from jax.experimental import pallas as pl
from jax.experimental.pallas import tpu as pltpu
from jax.sharding import PartitionSpec as P

NG = 96
SLAB_Y = 4
NPTS = 768
STEP = 8
VMEM = pl.BlockSpec(memory_space=pltpu.VMEM)


def device_number(x, y, z, core):
    val = x * 4 + (y // 4) * 2 + core
    return val * 32 + z * 4 + y % 4


def groups():
    out = []
    for first_y in (2, 6):
        for x0 in range(4):
            for core0 in range(2):
                members = [
                    device_number((z + t % 2 + x0) % 4, (first_y + t) % 8, z, (core0 + z // 4) % 2)
                    for z in range(8)
                    for t in range(4)
                ]
                out.append(members)
    return out


def whole_part(value, divisor):
    return jnp.floor((value + 0.5) * (1.0 / divisor))


def components(index):
    flat = index.astype(jnp.float32)
    a = whole_part(flat, NG * NG)
    rest = flat - a * (NG * NG)
    b = whole_part(rest, NG)
    return a, b, rest - b * NG


def cos_sin(a, b, c, x, y, z):
    turns = a * x + b * y + c * z
    turns = turns - NG * whole_part(turns, NG)
    angles = turns * (2.0 * math.pi / NG)
    return jnp.cos(angles), jnp.sin(angles)


def grid_points(shape, dim):
    points = lax.broadcasted_iota(jnp.int32, shape, dim).astype(jnp.float32)
    z = whole_part(points, NG * SLAB_Y)
    rest = points - z * (NG * SLAB_Y)
    y = whole_part(rest, NG)
    return rest - y * NG, y, z


def pack_kernel(val_ref, cond_ref, val_energy_ref, cond_energy_ref, index_ref, out_ref, own_ref):
    odd = lax.rem(lax.axis_index("cond"), 2) == 1
    val = val_ref[...].astype(jnp.float32)
    val = jnp.where(odd, val[2:4], val[0:2])
    a, b, c = components(index_ref[...])
    own_ref[...] = jnp.concatenate([a, b, c, jnp.zeros((5, 128), jnp.float32)], axis=0)
    energy = val_energy_ref[...].astype(jnp.float32)
    energy = jnp.where(odd, energy[:, 2:4], energy[:, 0:2])
    tail = jnp.concatenate(
        [cond_energy_ref[...].astype(jnp.float32), energy, jnp.zeros((1, 118), jnp.float32)], axis=1
    )
    rows = [val[h : h + 1, 256 * q : 256 * q + 256] for h in range(2) for q in range(3)]
    rows += [jnp.concatenate([a, b], axis=1), jnp.concatenate([c, tail], axis=1)]
    side = jnp.concatenate(rows, axis=0)
    block = jnp.concatenate([cond_ref[...].astype(jnp.float32), side], axis=1).astype(jnp.bfloat16)
    for k in range(out_ref.shape[0]):
        out_ref[k] = block


def dot(a, b, dims=(1, 0)):
    return lax.dot_general(
        a, b, (((dims[0],), (dims[1],)), ((), ())), preferred_element_type=jnp.float32
    )


def one_hot(condition):
    return jnp.where(condition, 1.0, 0.0).astype(jnp.bfloat16)


def iotas(rows, cols):
    return (
        lax.broadcasted_iota(jnp.int32, (rows, cols), 0),
        lax.broadcasted_iota(jnp.int32, (rows, cols), 1),
    )


def phase_table(a, b, c):
    x = lax.broadcasted_iota(jnp.int32, (NG, 1), 0).astype(jnp.float32)
    cos_x, sin_x = cos_sin(a, b, c, x, 0.0, 0.0)
    line = lax.broadcasted_iota(jnp.int32, (NPTS // NG, 1), 0).astype(jnp.float32)
    z = whole_part(line, SLAB_Y)
    cos_l, sin_l = cos_sin(a, b, c, 0.0, line - z * SLAB_Y, z)
    blocks = []
    for k in range(NPTS // NG):
        ck, sk = cos_l[k : k + 1], sin_l[k : k + 1]
        blocks.append(jnp.concatenate([cos_x * ck - sin_x * sk, sin_x * ck + cos_x * sk], axis=1).astype(jnp.bfloat16))
    return jnp.concatenate(blocks, axis=0)


def chi_kernel(factor, got_ref, own_ref, real_ref, imag_ref):
    conduction = got_ref[:, 0:NPTS]
    side = got_ref[:, NPTS:]

    row, lane = iotas(8, 128)
    mine = lane == row + 8 * lax.axis_index("val")
    head = got_ref[16:32, NPTS:].astype(jnp.float32)

    def own(values):
        return jnp.sum(jnp.where(mine, values, 0.0), axis=1, keepdims=True)

    a, b, c = own(head[6:7, 0:128]), own(head[6:7, 128:256]), own(head[7:8, 0:128])
    window = jnp.concatenate(cos_sin(a, b, c, *grid_points((8, NPTS), 1)), axis=0).astype(jnp.bfloat16)

    v, r = iotas(64, 256)
    first = 8 * (v // 2) + 3 * (v % 2)
    valence = jnp.concatenate([dot(one_hot(r == first + q), side) for q in range(3)], axis=1)
    narrow = valence.astype(jnp.bfloat16)
    energies = side[:, 128:256]
    picked = dot(one_hot(r == 8 * (v // 2) + 7), energies)
    v, l = iotas(64, 128)
    val_energy = jnp.sum(jnp.where(l == 8 + v % 2, picked, 0.0), axis=1, keepdims=True)
    r, k = iotas(256, 256)
    spread = dot(energies, one_hot(r == 8 * (k // 8) + 7), (0, 0))
    l, k = iotas(128, 256)
    cond_energy = jnp.sum(jnp.where(l == k % 8, spread, 0.0), axis=0, keepdims=True)
    weights = factor / (cond_energy - val_energy)

    lefts = [
        jnp.concatenate([narrow * window[j : j + 1, :] for j in range(start, start + STEP)], axis=0)
        for start in range(0, 16, STEP)
    ]
    totals = []
    ahead = dot(lefts[0], conduction, (1, 1))
    for following in [*lefts[1:], None]:
        terms = ahead
        if following is not None:
            ahead = dot(following, conduction, (1, 1))
        weighted = [(terms[64 * i : 64 * i + 64] * weights).astype(jnp.bfloat16) for i in range(STEP)]
        back = dot(jnp.concatenate(weighted, axis=0), conduction)
        totals += [jnp.sum(back[64 * i : 64 * i + 64] * valence, axis=0, keepdims=True) for i in range(STEP)]
    totals = jnp.concatenate(totals, axis=0)

    table = phase_table(own_ref[0:1], own_ref[1:2], own_ref[2:3])
    high = totals.astype(jnp.bfloat16)
    low = (totals - high.astype(jnp.float32)).astype(jnp.bfloat16)
    products = dot(high, table) + dot(low, table)
    real_ref[...] = products[0:8, 0:128] + products[8:16, 128:256]
    imag_ref[...] = products[0:8, 128:256] - products[8:16, 0:128]


def pack(val, cond, val_energy, cond_energy, index):
    return pl.pallas_call(
        pack_kernel,
        out_shape=[pltpu.VMEM((32, 8, 1024), jnp.bfloat16), pltpu.VMEM((8, 128), jnp.float32)],
        in_specs=[VMEM] * 5,
        out_specs=[VMEM] * 2,
    )(val, cond, val_energy, cond_energy, index)


def chi(got, own, factor):
    return pl.pallas_call(
        functools.partial(chi_kernel, factor),
        out_shape=[jax.ShapeDtypeStruct((8, 128), jnp.float32)] * 2,
        in_specs=[VMEM] * 2,
        out_specs=[VMEM] * 2,
        compiler_params=pltpu.CompilerParams(vmem_limit_bytes=32 * 1024 * 1024),
    )(got, own)


def per_device(val_orbitals, cond_orbitals, val_energy, cond_energy, wave_index):
    factor = -4.0 / math.sqrt(4 * lax.axis_size("val") * 8 * lax.axis_size("cond"))
    sent, own = pack(
        val_orbitals, cond_orbitals, val_energy.reshape(1, 4), cond_energy.reshape(1, 8), wave_index.reshape(1, 128)
    )
    got = lax.all_to_all(sent, ("val", "cond"), 0, 0, tiled=True, axis_index_groups=groups())
    return tuple(chi(got.reshape(256, 1024), own, factor))


def solution(mesh):
    return jax.shard_map(
        per_device,
        mesh=mesh,
        in_specs=(P("val", None), P("cond", None), P("val"), P("cond"), P("cond")),
        out_specs=(P("val", "cond"), P("val", "cond")),
        check_vma=False,
    )
```

```python
import functools
import math

import jax
import jax.numpy as jnp
from jax import lax
from jax.experimental import pallas as pl
from jax.experimental.pallas import tpu as pltpu
from jax.sharding import PartitionSpec as P

NG = 96
SLAB_Y = 4
NPTS = 768
STEP = 8
VMEM = pl.BlockSpec(memory_space=pltpu.VMEM)


def device_number(x, y, z, core):
    val = x * 4 + (y // 4) * 2 + core
    return val * 32 + z * 4 + y % 4


def groups():
    out = []
    for first_y in (2, 6):
        for x0 in range(4):
            for core0 in range(2):
                members = [
                    device_number((z + t % 2 + x0) % 4, (first_y + t) % 8, z, (core0 + z // 4) % 2)
                    for z in reversed(range(8))
                    for t in range(4)
                ]
                out.append(members)
    return out


def whole_part(value, divisor):
    return jnp.floor((value + 0.5) * (1.0 / divisor))


def components(index):
    flat = index.astype(jnp.float32)
    a = whole_part(flat, NG * NG)
    rest = flat - a * (NG * NG)
    b = whole_part(rest, NG)
    return a, b, rest - b * NG


def cos_sin(a, b, c, x, y, z):
    turns = a * x + b * y + c * z
    turns = turns - NG * whole_part(turns, NG)
    angles = turns * (2.0 * math.pi / NG)
    return jnp.cos(angles), jnp.sin(angles)


def grid_points(shape, dim):
    points = lax.broadcasted_iota(jnp.int32, shape, dim).astype(jnp.float32)
    z = whole_part(points, NG * SLAB_Y)
    rest = points - z * (NG * SLAB_Y)
    y = whole_part(rest, NG)
    return rest - y * NG, y, z


def pack_kernel(val_ref, cond_ref, val_energy_ref, cond_energy_ref, index_ref, out_ref, own_ref):
    odd = lax.rem(lax.axis_index("cond"), 2) == 1
    val = val_ref[...].astype(jnp.float32)
    val = jnp.where(odd, val[2:4], val[0:2])
    a, b, c = components(index_ref[...])
    own_ref[...] = jnp.concatenate([a, b, c, jnp.zeros((5, 128), jnp.float32)], axis=0)
    energy = val_energy_ref[...].astype(jnp.float32)
    energy = jnp.where(odd, energy[:, 2:4], energy[:, 0:2])
    tail = jnp.concatenate(
        [cond_energy_ref[...].astype(jnp.float32), energy, jnp.zeros((1, 118), jnp.float32)], axis=1
    )
    rows = [val[h : h + 1, 256 * q : 256 * q + 256] for h in range(2) for q in range(3)]
    rows += [jnp.concatenate([a, b], axis=1), jnp.concatenate([c, tail], axis=1)]
    side = jnp.concatenate(rows, axis=0)
    block = jnp.concatenate([cond_ref[...].astype(jnp.float32), side], axis=1).astype(jnp.bfloat16)
    for k in range(out_ref.shape[0]):
        out_ref[k] = block


def dot(a, b, dims=(1, 0)):
    return lax.dot_general(
        a, b, (((dims[0],), (dims[1],)), ((), ())), preferred_element_type=jnp.float32
    )


def one_hot(condition):
    return jnp.where(condition, 1.0, 0.0).astype(jnp.bfloat16)


def iotas(rows, cols):
    return (
        lax.broadcasted_iota(jnp.int32, (rows, cols), 0),
        lax.broadcasted_iota(jnp.int32, (rows, cols), 1),
    )


def phase_table(a, b, c):
    x = lax.broadcasted_iota(jnp.int32, (NG, 1), 0).astype(jnp.float32)
    cos_x, sin_x = cos_sin(a, b, c, x, 0.0, 0.0)
    line = lax.broadcasted_iota(jnp.int32, (NPTS // NG, 1), 0).astype(jnp.float32)
    z = whole_part(line, SLAB_Y)
    cos_l, sin_l = cos_sin(a, b, c, 0.0, line - z * SLAB_Y, z)
    blocks = []
    for k in range(NPTS // NG):
        ck, sk = cos_l[k : k + 1], sin_l[k : k + 1]
        blocks.append(jnp.concatenate([cos_x * ck - sin_x * sk, sin_x * ck + cos_x * sk], axis=1).astype(jnp.bfloat16))
    return jnp.concatenate(blocks, axis=0)


def chi_kernel(factor, got_ref, own_ref, real_ref, imag_ref):
    conduction = got_ref[:, 0:NPTS]
    side = got_ref[:, NPTS:]

    row, lane = iotas(8, 128)
    mine = lane == row + 8 * lax.axis_index("val")
    head = got_ref[240:256, NPTS:].astype(jnp.float32)

    def own(values):
        return jnp.sum(jnp.where(mine, values, 0.0), axis=1, keepdims=True)

    a, b, c = own(head[6:7, 0:128]), own(head[6:7, 128:256]), own(head[7:8, 0:128])
    window = jnp.concatenate(cos_sin(a, b, c, *grid_points((8, NPTS), 1)), axis=0).astype(jnp.bfloat16)

    v, r = iotas(64, 256)
    first = 8 * (v // 2) + 3 * (v % 2)
    valence = jnp.concatenate([dot(one_hot(r == first + q), side) for q in range(3)], axis=1)
    narrow = valence.astype(jnp.bfloat16)
    energies = side[:, 128:256]
    picked = dot(one_hot(r == 8 * (v // 2) + 7), energies)
    v, l = iotas(64, 128)
    val_energy = jnp.sum(jnp.where(l == 8 + v % 2, picked, 0.0), axis=1, keepdims=True)
    r, k = iotas(256, 256)
    spread = dot(energies, one_hot(r == 8 * (k // 8) + 7), (0, 0))
    l, k = iotas(128, 256)
    cond_energy = jnp.sum(jnp.where(l == k % 8, spread, 0.0), axis=0, keepdims=True)
    weights = factor / (cond_energy - val_energy)

    lefts = [
        jnp.concatenate([narrow * window[j : j + 1, :] for j in range(start, start + STEP)], axis=0)
        for start in range(0, 16, STEP)
    ]
    totals = []
    ahead = dot(lefts[0], conduction, (1, 1))
    for following in [*lefts[1:], None]:
        terms = ahead
        if following is not None:
            ahead = dot(following, conduction, (1, 1))
        weighted = [(terms[64 * i : 64 * i + 64] * weights).astype(jnp.bfloat16) for i in range(STEP)]
        back = dot(jnp.concatenate(weighted, axis=0), conduction)
        totals += [jnp.sum(back[64 * i : 64 * i + 64] * valence, axis=0, keepdims=True) for i in range(STEP)]
    totals = jnp.concatenate(totals, axis=0)

    table = phase_table(own_ref[0:1], own_ref[1:2], own_ref[2:3])
    high = totals.astype(jnp.bfloat16)
    low = (totals - high.astype(jnp.float32)).astype(jnp.bfloat16)
    products = dot(high, table) + dot(low, table)
    real_ref[...] = products[0:8, 0:128] + products[8:16, 128:256]
    imag_ref[...] = products[0:8, 128:256] - products[8:16, 0:128]


def pack(val, cond, val_energy, cond_energy, index):
    return pl.pallas_call(
        pack_kernel,
        out_shape=[pltpu.VMEM((32, 8, 1024), jnp.bfloat16), pltpu.VMEM((8, 128), jnp.float32)],
        in_specs=[VMEM] * 5,
        out_specs=[VMEM] * 2,
    )(val, cond, val_energy, cond_energy, index)


def chi(got, own, factor):
    return pl.pallas_call(
        functools.partial(chi_kernel, factor),
        out_shape=[jax.ShapeDtypeStruct((8, 128), jnp.float32)] * 2,
        in_specs=[VMEM] * 2,
        out_specs=[VMEM] * 2,
        compiler_params=pltpu.CompilerParams(vmem_limit_bytes=32 * 1024 * 1024),
    )(got, own)


def per_device(val_orbitals, cond_orbitals, val_energy, cond_energy, wave_index):
    factor = -4.0 / math.sqrt(4 * lax.axis_size("val") * 8 * lax.axis_size("cond"))
    sent, own = pack(
        val_orbitals, cond_orbitals, val_energy.reshape(1, 4), cond_energy.reshape(1, 8), wave_index.reshape(1, 128)
    )
    got = lax.all_to_all(sent, ("val", "cond"), 0, 0, tiled=True, axis_index_groups=groups())
    return tuple(chi(got.reshape(256, 1024), own, factor))


def solution(mesh):
    return jax.shard_map(
        per_device,
        mesh=mesh,
        in_specs=(P("val", None), P("cond", None), P("val"), P("cond"), P("cond")),
        out_specs=(P("val", "cond"), P("val", "cond")),
        check_vma=False,
    )
```

```python
import functools
import math

import jax
import jax.numpy as jnp
from jax import lax
from jax.experimental import pallas as pl
from jax.experimental.pallas import tpu as pltpu
from jax.sharding import PartitionSpec as P

NG = 96
SLAB_Y = 4
NPTS = 768
STEP = 8
VMEM = pl.BlockSpec(memory_space=pltpu.VMEM)


def device_number(x, y, z, core):
    val = x * 4 + (y // 4) * 2 + core
    return val * 32 + z * 4 + y % 4


def groups():
    out = []
    for first_y, order in ((2, (2, 3, 0, 1)), (6, (0, 1, 2, 3))):
        for x0 in range(4):
            for core0 in range(2):
                members = [
                    device_number((z + t % 2 + x0) % 4, (first_y + t) % 8, z, (core0 + z // 4) % 2)
                    for z in reversed(range(8))
                    for t in order
                ]
                out.append(members)
    return out


def whole_part(value, divisor):
    return jnp.floor((value + 0.5) * (1.0 / divisor))


def components(index):
    flat = index.astype(jnp.float32)
    a = whole_part(flat, NG * NG)
    rest = flat - a * (NG * NG)
    b = whole_part(rest, NG)
    return a, b, rest - b * NG


def cos_sin(a, b, c, x, y, z):
    turns = a * x + b * y + c * z
    turns = turns - NG * whole_part(turns, NG)
    angles = turns * (2.0 * math.pi / NG)
    return jnp.cos(angles), jnp.sin(angles)


def grid_points(shape, dim):
    points = lax.broadcasted_iota(jnp.int32, shape, dim).astype(jnp.float32)
    z = whole_part(points, NG * SLAB_Y)
    rest = points - z * (NG * SLAB_Y)
    y = whole_part(rest, NG)
    return rest - y * NG, y, z


def pack_kernel(val_ref, cond_ref, val_energy_ref, cond_energy_ref, index_ref, out_ref, own_ref):
    odd = lax.rem(lax.axis_index("cond"), 2) == 1
    val = val_ref[...].astype(jnp.float32)
    val = jnp.where(odd, val[2:4], val[0:2])
    a, b, c = components(index_ref[...])
    own_ref[...] = jnp.concatenate([a, b, c, jnp.zeros((5, 128), jnp.float32)], axis=0)
    energy = val_energy_ref[...].astype(jnp.float32)
    energy = jnp.where(odd, energy[:, 2:4], energy[:, 0:2])
    tail = jnp.concatenate(
        [cond_energy_ref[...].astype(jnp.float32), energy, jnp.zeros((1, 118), jnp.float32)], axis=1
    )
    rows = [val[h : h + 1, 256 * q : 256 * q + 256] for h in range(2) for q in range(3)]
    rows += [jnp.concatenate([a, b], axis=1), jnp.concatenate([c, tail], axis=1)]
    side = jnp.concatenate(rows, axis=0)
    block = jnp.concatenate([cond_ref[...].astype(jnp.float32), side], axis=1).astype(jnp.bfloat16)
    for k in range(out_ref.shape[0]):
        out_ref[k] = block


def dot(a, b, dims=(1, 0)):
    return lax.dot_general(
        a, b, (((dims[0],), (dims[1],)), ((), ())), preferred_element_type=jnp.float32
    )


def one_hot(condition):
    return jnp.where(condition, 1.0, 0.0).astype(jnp.bfloat16)


def iotas(rows, cols):
    return (
        lax.broadcasted_iota(jnp.int32, (rows, cols), 0),
        lax.broadcasted_iota(jnp.int32, (rows, cols), 1),
    )


def phase_table(a, b, c):
    x = lax.broadcasted_iota(jnp.int32, (NG, 1), 0).astype(jnp.float32)
    cos_x, sin_x = cos_sin(a, b, c, x, 0.0, 0.0)
    line = lax.broadcasted_iota(jnp.int32, (NPTS // NG, 1), 0).astype(jnp.float32)
    z = whole_part(line, SLAB_Y)
    cos_l, sin_l = cos_sin(a, b, c, 0.0, line - z * SLAB_Y, z)
    blocks = []
    for k in range(NPTS // NG):
        ck, sk = cos_l[k : k + 1], sin_l[k : k + 1]
        blocks.append(jnp.concatenate([cos_x * ck - sin_x * sk, sin_x * ck + cos_x * sk], axis=1).astype(jnp.bfloat16))
    return jnp.concatenate(blocks, axis=0)


def chi_kernel(factor, got_ref, own_ref, real_ref, imag_ref):
    conduction = got_ref[:, 0:NPTS]
    side = got_ref[:, NPTS:]

    row, lane = iotas(8, 128)
    mine = lane == row + 8 * lax.axis_index("val")
    y_high, y_low = lax.rem(lax.axis_index("val") // 2, 2), lax.rem(lax.axis_index("cond"), 4)
    middle = (y_high == 0) == (y_low >= 2)
    last = got_ref[224:256, NPTS:].astype(jnp.float32)
    head = jnp.where(middle, last[0:16], last[16:32])

    def own(values):
        return jnp.sum(jnp.where(mine, values, 0.0), axis=1, keepdims=True)

    a, b, c = own(head[6:7, 0:128]), own(head[6:7, 128:256]), own(head[7:8, 0:128])
    window = jnp.concatenate(cos_sin(a, b, c, *grid_points((8, NPTS), 1)), axis=0).astype(jnp.bfloat16)

    v, r = iotas(64, 256)
    first = 8 * (v // 2) + 3 * (v % 2)
    valence = jnp.concatenate([dot(one_hot(r == first + q), side) for q in range(3)], axis=1)
    narrow = valence.astype(jnp.bfloat16)
    energies = side[:, 128:256]
    picked = dot(one_hot(r == 8 * (v // 2) + 7), energies)
    v, l = iotas(64, 128)
    val_energy = jnp.sum(jnp.where(l == 8 + v % 2, picked, 0.0), axis=1, keepdims=True)
    r, k = iotas(256, 256)
    spread = dot(energies, one_hot(r == 8 * (k // 8) + 7), (0, 0))
    l, k = iotas(128, 256)
    cond_energy = jnp.sum(jnp.where(l == k % 8, spread, 0.0), axis=0, keepdims=True)
    weights = factor / (cond_energy - val_energy)

    lefts = [
        jnp.concatenate([narrow * window[j : j + 1, :] for j in range(start, start + STEP)], axis=0)
        for start in range(0, 16, STEP)
    ]
    totals = []
    ahead = dot(lefts[0], conduction, (1, 1))
    for following in [*lefts[1:], None]:
        terms = ahead
        if following is not None:
            ahead = dot(following, conduction, (1, 1))
        weighted = [(terms[64 * i : 64 * i + 64] * weights).astype(jnp.bfloat16) for i in range(STEP)]
        back = dot(jnp.concatenate(weighted, axis=0), conduction)
        totals += [jnp.sum(back[64 * i : 64 * i + 64] * valence, axis=0, keepdims=True) for i in range(STEP)]
    totals = jnp.concatenate(totals, axis=0)

    table = phase_table(own_ref[0:1], own_ref[1:2], own_ref[2:3])
    high = totals.astype(jnp.bfloat16)
    low = (totals - high.astype(jnp.float32)).astype(jnp.bfloat16)
    products = dot(high, table) + dot(low, table)
    real_ref[...] = products[0:8, 0:128] + products[8:16, 128:256]
    imag_ref[...] = products[0:8, 128:256] - products[8:16, 0:128]


def pack(val, cond, val_energy, cond_energy, index):
    return pl.pallas_call(
        pack_kernel,
        out_shape=[pltpu.VMEM((32, 8, 1024), jnp.bfloat16), pltpu.VMEM((8, 128), jnp.float32)],
        in_specs=[VMEM] * 5,
        out_specs=[VMEM] * 2,
    )(val, cond, val_energy, cond_energy, index)


def chi(got, own, factor):
    return pl.pallas_call(
        functools.partial(chi_kernel, factor),
        out_shape=[jax.ShapeDtypeStruct((8, 128), jnp.float32)] * 2,
        in_specs=[VMEM] * 2,
        out_specs=[VMEM] * 2,
        compiler_params=pltpu.CompilerParams(vmem_limit_bytes=32 * 1024 * 1024),
    )(got, own)


def per_device(val_orbitals, cond_orbitals, val_energy, cond_energy, wave_index):
    factor = -4.0 / math.sqrt(4 * lax.axis_size("val") * 8 * lax.axis_size("cond"))
    sent, own = pack(
        val_orbitals, cond_orbitals, val_energy.reshape(1, 4), cond_energy.reshape(1, 8), wave_index.reshape(1, 128)
    )
    got = lax.all_to_all(sent, ("val", "cond"), 0, 0, tiled=True, axis_index_groups=groups())
    return tuple(chi(got.reshape(256, 1024), own, factor))


def solution(mesh):
    return jax.shard_map(
        per_device,
        mesh=mesh,
        in_specs=(P("val", None), P("cond", None), P("val"), P("cond"), P("cond")),
        out_specs=(P("val", "cond"), P("val", "cond")),
        check_vma=False,
    )
```

```python
import functools
import math

import jax
import jax.numpy as jnp
from jax import lax
from jax.experimental import pallas as pl
from jax.experimental.pallas import tpu as pltpu
from jax.sharding import PartitionSpec as P

NG = 96
SLAB_Y = 4
NPTS = 768
STEP = 8
VMEM = pl.BlockSpec(memory_space=pltpu.VMEM)


def device_number(x, y, z, core):
    val = x * 4 + (y // 4) * 2 + core
    return val * 32 + z * 4 + y % 4


def groups():
    out = []
    for first_y, order in ((2, (2, 3, 1, 0)), (6, (0, 1, 3, 2))):
        for x0 in range(4):
            for core0 in range(2):
                members = [
                    device_number((z + t % 2 + x0) % 4, (first_y + t) % 8, z, (core0 + z // 4) % 2)
                    for z in reversed(range(8))
                    for t in order
                ]
                out.append(members)
    return out


def whole_part(value, divisor):
    return jnp.floor((value + 0.5) * (1.0 / divisor))


def components(index):
    flat = index.astype(jnp.float32)
    a = whole_part(flat, NG * NG)
    rest = flat - a * (NG * NG)
    b = whole_part(rest, NG)
    return a, b, rest - b * NG


def cos_sin(a, b, c, x, y, z):
    turns = a * x + b * y + c * z
    turns = turns - NG * whole_part(turns, NG)
    angles = turns * (2.0 * math.pi / NG)
    return jnp.cos(angles), jnp.sin(angles)


def grid_points(shape, dim):
    points = lax.broadcasted_iota(jnp.int32, shape, dim).astype(jnp.float32)
    z = whole_part(points, NG * SLAB_Y)
    rest = points - z * (NG * SLAB_Y)
    y = whole_part(rest, NG)
    return rest - y * NG, y, z


def pack_kernel(val_ref, cond_ref, val_energy_ref, cond_energy_ref, index_ref, out_ref, own_ref):
    odd = lax.rem(lax.axis_index("cond"), 2) == 1
    val = val_ref[...].astype(jnp.float32)
    val = jnp.where(odd, val[2:4], val[0:2])
    a, b, c = components(index_ref[...])
    own_ref[...] = jnp.concatenate([a, b, c, jnp.zeros((5, 128), jnp.float32)], axis=0)
    energy = val_energy_ref[...].astype(jnp.float32)
    energy = jnp.where(odd, energy[:, 2:4], energy[:, 0:2])
    tail = jnp.concatenate(
        [cond_energy_ref[...].astype(jnp.float32), energy, jnp.zeros((1, 118), jnp.float32)], axis=1
    )
    rows = [val[h : h + 1, 256 * q : 256 * q + 256] for h in range(2) for q in range(3)]
    rows += [jnp.concatenate([a, b], axis=1), jnp.concatenate([c, tail], axis=1)]
    side = jnp.concatenate(rows, axis=0)
    block = jnp.concatenate([cond_ref[...].astype(jnp.float32), side], axis=1).astype(jnp.bfloat16)
    for k in range(out_ref.shape[0]):
        out_ref[k] = block


def dot(a, b, dims=(1, 0)):
    return lax.dot_general(
        a, b, (((dims[0],), (dims[1],)), ((), ())), preferred_element_type=jnp.float32
    )


def one_hot(condition):
    return jnp.where(condition, 1.0, 0.0).astype(jnp.bfloat16)


def iotas(rows, cols):
    return (
        lax.broadcasted_iota(jnp.int32, (rows, cols), 0),
        lax.broadcasted_iota(jnp.int32, (rows, cols), 1),
    )


def phase_table(a, b, c):
    x = lax.broadcasted_iota(jnp.int32, (NG, 1), 0).astype(jnp.float32)
    cos_x, sin_x = cos_sin(a, b, c, x, 0.0, 0.0)
    line = lax.broadcasted_iota(jnp.int32, (NPTS // NG, 1), 0).astype(jnp.float32)
    z = whole_part(line, SLAB_Y)
    cos_l, sin_l = cos_sin(a, b, c, 0.0, line - z * SLAB_Y, z)
    blocks = []
    for k in range(NPTS // NG):
        ck, sk = cos_l[k : k + 1], sin_l[k : k + 1]
        blocks.append(jnp.concatenate([cos_x * ck - sin_x * sk, sin_x * ck + cos_x * sk], axis=1).astype(jnp.bfloat16))
    return jnp.concatenate(blocks, axis=0)


def chi_kernel(factor, got_ref, own_ref, real_ref, imag_ref):
    conduction = got_ref[:, 0:NPTS]
    side = got_ref[:, NPTS:]

    row, lane = iotas(8, 128)
    mine = lane == row + 8 * lax.axis_index("val")
    y_high, y_low = lax.rem(lax.axis_index("val") // 2, 2), lax.rem(lax.axis_index("cond"), 4)
    middle = (y_high == 0) == (y_low >= 2)
    last = got_ref[224:256, NPTS:].astype(jnp.float32)
    head = jnp.where(middle, last[0:8], last[24:32])

    def own(values):
        return jnp.sum(jnp.where(mine, values, 0.0), axis=1, keepdims=True)

    a, b, c = own(head[6:7, 0:128]), own(head[6:7, 128:256]), own(head[7:8, 0:128])
    window = jnp.concatenate(cos_sin(a, b, c, *grid_points((8, NPTS), 1)), axis=0).astype(jnp.bfloat16)

    v, r = iotas(64, 256)
    first = 8 * (v // 2) + 3 * (v % 2)
    valence = jnp.concatenate([dot(one_hot(r == first + q), side) for q in range(3)], axis=1)
    narrow = valence.astype(jnp.bfloat16)
    energies = side[:, 128:256]
    picked = dot(one_hot(r == 8 * (v // 2) + 7), energies)
    v, l = iotas(64, 128)
    val_energy = jnp.sum(jnp.where(l == 8 + v % 2, picked, 0.0), axis=1, keepdims=True)
    r, k = iotas(256, 256)
    spread = dot(energies, one_hot(r == 8 * (k // 8) + 7), (0, 0))
    l, k = iotas(128, 256)
    cond_energy = jnp.sum(jnp.where(l == k % 8, spread, 0.0), axis=0, keepdims=True)
    weights = factor / (cond_energy - val_energy)

    lefts = [
        jnp.concatenate([narrow * window[j : j + 1, :] for j in range(start, start + STEP)], axis=0)
        for start in range(0, 16, STEP)
    ]
    totals = []
    ahead = dot(lefts[0], conduction, (1, 1))
    for following in [*lefts[1:], None]:
        terms = ahead
        if following is not None:
            ahead = dot(following, conduction, (1, 1))
        weighted = [(terms[64 * i : 64 * i + 64] * weights).astype(jnp.bfloat16) for i in range(STEP)]
        back = dot(jnp.concatenate(weighted, axis=0), conduction)
        totals += [jnp.sum(back[64 * i : 64 * i + 64] * valence, axis=0, keepdims=True) for i in range(STEP)]
    totals = jnp.concatenate(totals, axis=0)

    table = phase_table(own_ref[0:1], own_ref[1:2], own_ref[2:3])
    high = totals.astype(jnp.bfloat16)
    low = (totals - high.astype(jnp.float32)).astype(jnp.bfloat16)
    products = dot(high, table) + dot(low, table)
    real_ref[...] = products[0:8, 0:128] + products[8:16, 128:256]
    imag_ref[...] = products[0:8, 128:256] - products[8:16, 0:128]


def pack(val, cond, val_energy, cond_energy, index):
    return pl.pallas_call(
        pack_kernel,
        out_shape=[pltpu.VMEM((32, 8, 1024), jnp.bfloat16), pltpu.VMEM((8, 128), jnp.float32)],
        in_specs=[VMEM] * 5,
        out_specs=[VMEM] * 2,
    )(val, cond, val_energy, cond_energy, index)


def chi(got, own, factor):
    return pl.pallas_call(
        functools.partial(chi_kernel, factor),
        out_shape=[jax.ShapeDtypeStruct((8, 128), jnp.float32)] * 2,
        in_specs=[VMEM] * 2,
        out_specs=[VMEM] * 2,
        compiler_params=pltpu.CompilerParams(vmem_limit_bytes=32 * 1024 * 1024),
    )(got, own)


def per_device(val_orbitals, cond_orbitals, val_energy, cond_energy, wave_index):
    factor = -4.0 / math.sqrt(4 * lax.axis_size("val") * 8 * lax.axis_size("cond"))
    sent, own = pack(
        val_orbitals, cond_orbitals, val_energy.reshape(1, 4), cond_energy.reshape(1, 8), wave_index.reshape(1, 128)
    )
    got = lax.all_to_all(sent, ("val", "cond"), 0, 0, tiled=True, axis_index_groups=groups())
    return tuple(chi(got.reshape(256, 1024), own, factor))


def solution(mesh):
    return jax.shard_map(
        per_device,
        mesh=mesh,
        in_specs=(P("val", None), P("cond", None), P("val"), P("cond"), P("cond")),
        out_specs=(P("val", "cond"), P("val", "cond")),
        check_vma=False,
    )
```
